32 devices in a mesh: groups: 2 (over x), expert: 16 (over z, y, core).
Axes of the slice: x: 2, y: 2, z: 4, core: 2. Of those that a mesh axis runs over, the one named last changes fastest.
Arguments:
- hidden_in: bfloat16 [512, 4096], P(('groups', 'expert')), parts along dimension 0, may hold values from -6 to 6
- norm_gain: float32 [4096], replicated, may hold values from 0.5 to 1.5
- router_weight: bfloat16 [4096, 4], replicated, may hold values from -0.09375 to 0.09375
- expert_ids: int32 [512, 2], P(('groups', 'expert')), parts along dimension 0, may hold values from 0 to 3, all different within a row; in each aligned block of 8 rows (0 to 7, 8 to 15, ...) at most 6 rows name the same one
- up_weight: bfloat16 [4096, 49152], P(None, 'expert'), may hold values from -0.09375 to 0.09375
- down_weight: bfloat16 [49152, 4096], P('expert'), may hold values from -0.0546875 to 0.0546875
Outputs:
- mixed_out: bfloat16 [512, 4096], P(('groups', 'expert')), parts along dimension 0
The draws below stay inside these ranges and needn't reach their ends.
There are 2 independent parts, one for each index of `groups`. The reference program is written for one: setup_inputs(seed, part) draws one part's arguments, and reference() takes and returns one part's arrays. A program takes and returns all parts, laid end to end along the dimension named above; an argument that names none is the same for every part. Nothing has to cross between parts.
Inputs may be any that keep to these rules, and one draw needn't show every extreme that they name: `expert_ids`: each row names two different experts. Rows form aligned blocks of 8 rows (one micro-batch of one device); in each block no expert is named by more than 6 rows, and in some blocks one expert is named by exactly 6 rows.
All inputs are finite; a program needn't handle non-finite values.
Results may differ from the reference program's by a relative error of at most 0.0037.
Values may be sent and summed in bfloat16 or wider, within the bound.
A program may use at most 128 MiB of HBM per device.

```python
import math
import jax
import jax.numpy as jnp
import numpy as np
from jax import lax

D = 4096
FF = 12288
EXPERTS = 4
MB_ROWS = 8
CAP = 6
TOKENS = 256


def shard_levels(rng, shape, cuts, low, top_value):
    loudness = 1.0
    for dim, blocks in cuts:
        heights = jax.random.uniform(jax.random.fold_in(jax.random.fold_in(rng, 6), dim), (blocks,), jnp.float32, low / len(cuts), top_value / len(cuts))
        loudness = loudness * jnp.repeat(jnp.exp(heights), shape[dim] // blocks).reshape((-1,) + (1,) * (len(shape) - 1 - dim))
    return loudness


def routed_block(own_key, own, number, rows, number_of, top, bound, skew):
    ranking = jax.random.permutation(own_key, number_of)
    heavy_load, ordinary = portions_of(number_of, rows * top, bound, skew, True), portions_of(number_of, rows * top, bound, skew, False)
    places = jnp.arange(number_of)

    def named(lengths, offset_by):
        used = int((lengths > 0).sum())
        fixed = max(1, used // 4)
        shifted = fixed + (places - fixed + offset_by * (used - fixed)) % max(1, number_of - fixed)
        return jnp.zeros((number_of,), jnp.int32).at[ranking[jnp.where(places < fixed, places, shifted)]].set(jnp.asarray(lengths, jnp.int32))

    lengths = jnp.where(number % 4 == 0, named(heavy_load, number // 4), named(ordinary, number - number // 4 - 1))
    mixed = jax.random.permutation(jax.random.fold_in(own, 3), number_of)
    source_of, receiver = mixed[0:number_of // 2 * 2:2], mixed[1:number_of // 2 * 2:2]
    margin = jnp.minimum(lengths[source_of] - 1, bound - lengths[receiver]) // 2
    margin = jnp.where((source_of == ranking[0]) | (receiver == ranking[0]) | (lengths[receiver] == 0), 0, jnp.maximum(margin, 0))
    shifted = jax.random.randint(jax.random.fold_in(own, 4), (number_of // 2,), 0, 1 << 20) % (margin + 1)
    lengths = lengths.at[source_of].add(-shifted).at[receiver].add(shifted)
    items = jnp.searchsorted(jnp.cumsum(lengths), jnp.arange(rows * top), side="right").astype(jnp.int32)
    grid = items.reshape(top, rows).T
    grid = grid[jax.random.permutation(jax.random.fold_in(own, 1), rows)]
    offset_by = jax.random.randint(jax.random.fold_in(own, 2), (rows, 1), 0, top)
    return jnp.take_along_axis(grid, (jnp.arange(top)[None, :] + offset_by) % top, axis=1)


def portions_of(count, total, limit, lean, full):
    weights = [(1 << 20) // math.isqrt(grade ** lean) + 1 for grade in range(1, count + 1)]
    largest = limit if full else min(limit, max(-(-total // count), total * weights[0] // sum(weights)))
    least = 1 if total - largest >= count - 1 else 0
    given, spare = [largest] + [least] * (count - 1), total - largest - least * (count - 1)
    while spare > 0:
        movable = [i for i in range(1, count) if given[i] < largest] or [i for i in range(1, count) if given[i] < limit]
        whole, budget = sum([weights[i] for i in movable]), spare
        for i in movable:
            extra = min(limit - given[i], max(1, budget * weights[i] // whole), spare)
            given[i] = given[i] + extra
            spare = spare - extra
    return np.array(given)


def gaussian(own_key, dims, scale, most, cuts=(), held_as=jnp.bfloat16):
    values = scale * jax.random.normal(own_key, dims, jnp.float32)
    if cuts:
        values = values * shard_levels(own_key, dims, cuts, -0.22, 0.18)
    return jnp.clip(values, -most, most).astype(held_as)


def setup_inputs(seed: int = 0, part: int = 0) -> dict:
    keys = jax.random.split(jax.random.key(seed), 7)
    part_keys = jax.random.split(jax.random.fold_in(keys[6], part), 7)
    hidden_in = gaussian(part_keys[0], (TOKENS, D), 1.0, 6.0, ((0, 16),))
    norm_gain = jnp.clip(1.0 + 0.1 * jax.random.normal(keys[1], (D,), jnp.float32), 0.5, 1.5)
    router_weight = gaussian(keys[2], (D, EXPERTS), D ** -0.5, 0.09375)
    expert_ids_keys = jax.random.split(jax.random.fold_in(part_keys[3], 1), TOKENS // MB_ROWS)
    expert_ids_turns = jax.random.permutation(jax.random.fold_in(part_keys[3], 3), TOKENS // MB_ROWS)
    expert_ids = jax.vmap(lambda own, number: routed_block(jax.random.fold_in(part_keys[3], 2), own, number, MB_ROWS, EXPERTS, 2, CAP, 2))(expert_ids_keys, expert_ids_turns).reshape((TOKENS, 2))
    up_weight = gaussian(keys[4], (D, EXPERTS * FF), D ** -0.5, 0.09375, ((1, 16),))
    down_weight = gaussian(keys[5], (EXPERTS * FF, D), FF ** -0.5, 0.0546875, ((0, 16),))
    return {"hidden_in": hidden_in, "norm_gain": norm_gain, "router_weight": router_weight, "expert_ids": expert_ids, "up_weight": up_weight, "down_weight": down_weight}


def rms_norm(hidden_in, norm_gain):
    values = hidden_in.astype(jnp.float32)
    scale = lax.rsqrt(lax.optimization_barrier(jnp.mean(values * values, axis=1, keepdims=True)) + 1e-05)
    return (values * scale * norm_gain[None, :]).astype(jnp.bfloat16)

def pair_mix(logits, expert_ids):
    labels = jnp.arange(logits.shape[1], dtype=jnp.int32)
    match = expert_ids[:, :, None] == labels[None, None, :]
    picked = lax.optimization_barrier(jnp.sum(jnp.where(match, logits[:, None, :], 0.0), axis=2))
    return 1.0 / (1.0 + jnp.exp(picked[:, ::-1] - picked))

def reference(hidden_in, norm_gain, router_weight, expert_ids, up_weight, down_weight):
    normed = rms_norm(hidden_in, norm_gain)
    logits = jnp.dot(normed, router_weight, preferred_element_type=jnp.float32)
    mix = pair_mix(logits, expert_ids)
    total = jnp.zeros(hidden_in.shape, jnp.float32)
    for expert in range(EXPERTS):
        columns = up_weight[:, expert * FF:(expert + 1) * FF]
        hidden = jax.nn.silu(jnp.dot(normed, columns, preferred_element_type=jnp.float32)).astype(jnp.bfloat16)
        result = jnp.dot(hidden, down_weight[expert * FF:(expert + 1) * FF, :], preferred_element_type=jnp.float32)
        factor = lax.optimization_barrier(jnp.sum(jnp.where(expert_ids == expert, mix, 0.0), axis=1))
        total = total + factor[:, None] * result
    return (hidden_in.astype(jnp.float32) + total).astype(jnp.bfloat16)
```

```python
import functools

import jax
import jax.numpy as jnp
from jax import lax
from jax.experimental import pallas as pl
from jax.experimental.pallas import tpu as pltpu
from jax.sharding import PartitionSpec as P

MESH = pl.DeviceIdType.MESH
BF = jnp.bfloat16
F32 = jnp.float32
EXTRA = 128


def tile_of(size):
    for tile in (512, 384, 256, 128):
        if size % tile == 0:
            return tile
    return size


def kernel(
    devices, experts, hid_ref, gain_ref, router_ref, ids_ref, up_ref, down_ref, out_ref,
    rows_buf, up_buf, down_buf, hidden_buf, part, from_core, from_peer, from_plane, factor_buf,
    up_sem, down_sem, d1_send, d1_recv, d2_send, d2_recv, d3_send, d3_recv,
    r1_send, r1_recv, r2_send, r2_recv, r3_send, r3_recv,
):
    group = devices // experts
    peers = group // 2
    rows, width = hid_ref.shape
    ups, _, up_tile = up_buf.shape
    downs, _, down_tile = down_buf.shape
    half = experts * peers * rows
    span = experts * rows
    me = lax.axis_index("expert")
    plane = me // group
    peer = lax.rem(me, group) // 2
    core = lax.rem(me, 2)

    def index(p, h, c):
        return p * group + h * 2 + c

    def place(p, h, c):
        return pl.multiple_of(((c * peers + h) * experts + p) * rows, rows)

    def other_plane(step):
        return lax.rem(plane + step, experts)

    def source_plane(step):
        return lax.rem(plane + experts - step, experts)

    def other_peer(step):
        return lax.rem(peer + step, peers)

    def source_peer(step):
        return lax.rem(peer + peers - step, peers)

    def remote(src, dst, send, recv, target):
        return pltpu.make_async_remote_copy(
            src_ref=src, dst_ref=dst, send_sem=send, recv_sem=recv,
            device_id={"expert": target}, device_id_type=MESH,
        )

    def up_copy(i):
        return pltpu.make_async_copy(
            up_ref.at[:, pl.ds(pl.multiple_of(i * up_tile, up_tile), up_tile)], up_buf.at[i], up_sem.at[i]
        )

    def down_copy(i):
        return pltpu.make_async_copy(
            down_ref.at[:, pl.ds(pl.multiple_of(i * down_tile, down_tile), down_tile)],
            down_buf.at[i], down_sem.at[i],
        )

    barrier = pltpu.get_barrier_semaphore()
    friends = [index(other_plane(s), peer, core) for s in range(1, experts)]
    friends += [index(plane, other_peer(s), core) for s in range(1, peers)]
    friends += [index(plane, peer, 1 - core)]
    for friend in friends:
        pl.semaphore_signal(barrier, inc=1, device_id={"expert": friend}, device_id_type=MESH)

    for i in range(ups):
        up_copy(i).start()
    for i in range(downs):
        down_copy(i).start()

    values = hid_ref[...].astype(F32)
    scale = lax.rsqrt(jnp.mean(values * values, axis=1, keepdims=True) + 1e-05)
    normed = (values * scale * gain_ref[...]).astype(BF)
    own = pl.ds(place(plane, peer, core), rows)
    rows_buf[own, :width] = normed
    normed32 = normed.astype(F32)
    router = router_ref[...].astype(F32)
    logits = [jnp.sum(normed32 * router[e:e + 1, :], axis=1, keepdims=True) for e in range(experts)]
    first, second = ids_ref[:, 0:1], ids_ref[:, 1:2]
    picked = [
        sum(jnp.where(ids == e, logits[e], 0.0) for e in range(experts)) for ids in (first, second)
    ]
    mix0 = 1.0 / (1.0 + jnp.exp(picked[1] - picked[0]))
    mix1 = 1.0 / (1.0 + jnp.exp(picked[0] - picked[1]))
    lane = lax.broadcasted_iota(jnp.int32, (rows, EXTRA), 1)
    label = lax.rem(lane, experts)
    factor = jnp.where(first == label, mix0, 0.0) + jnp.where(second == label, mix1, 0.0)
    high = factor.astype(BF)
    low = (factor - high.astype(F32)).astype(BF)
    rows_buf[own, width:] = jnp.where(
        lane < experts, high.astype(F32), jnp.where(lane < 2 * experts, low.astype(F32), 0.0)
    ).astype(BF)

    pl.semaphore_wait(barrier, len(friends))

    def block(p, h, c):
        return rows_buf.at[pl.ds(place(p, h, c), rows)]

    def d1(step):
        b = block(plane, peer, core)
        return remote(b, b, d1_send.at[step - 1], d1_recv.at[step - 1],
                      index(other_plane(step), peer, core))

    def d2(j, step):
        b = block(source_plane(step), peer, core)
        return remote(b, b, d2_send.at[j - 1, step], d2_recv.at[j - 1, step],
                      index(plane, other_peer(j), core))

    def d3(j, step):
        b = block(source_plane(step), source_peer(j), core)
        return remote(b, b, d3_send.at[j, step], d3_recv.at[j, step],
                      index(plane, peer, 1 - core))

    for step in range(1, experts):
        d1(step).start()
    for step in range(experts):
        if step:
            d1(step).wait_recv()
        for j in range(1, peers):
            d2(j, step).start()
        d3(0, step).start()
    for step in range(experts):
        for j in range(1, peers):
            d2(j, step).wait_recv()
            d3(j, step).start()
    for step in range(experts):
        for j in range(peers):
            d3(j, step).wait_recv()

    lane_all = lax.broadcasted_iota(jnp.int32, (2 * half, EXTRA), 1)
    chosen = (lane_all == plane) | (lane_all == plane + experts)
    factor_buf[...] = jnp.broadcast_to(
        jnp.sum(jnp.where(chosen, rows_buf[:, width:].astype(F32), 0.0), axis=1, keepdims=True),
        factor_buf.shape,
    )

    @pl.loop(0, ups)
    def _(i):
        up_copy(i).wait()
        value = jnp.dot(rows_buf[:, :width], up_buf[i], preferred_element_type=F32)
        hidden_buf[:, pl.ds(pl.multiple_of(i * up_tile, up_tile), up_tile)] = (
            value / (1.0 + jnp.exp(-value))
        ).astype(BF)

    base = pl.multiple_of(core * half, rows)
    away = pl.multiple_of((1 - core) * half, rows)
    mine = pl.multiple_of(base + peer * span, rows)
    final = pl.multiple_of(mine + plane * rows, rows)

    def r1(k):
        return remote(part.at[k, pl.ds(away, half)], from_core.at[k], r1_send.at[k], r1_recv.at[k],
                      index(plane, peer, 1 - core))

    def r2(k, j):
        start = pl.multiple_of(base + other_peer(j) * span, rows)
        return remote(part.at[k, pl.ds(start, span)], from_peer.at[k, j - 1],
                      r2_send.at[k, j - 1], r2_recv.at[k, j - 1],
                      index(plane, other_peer(j), core))

    def r3(k, step):
        start = pl.multiple_of(mine + other_plane(step) * rows, rows)
        return remote(part.at[k, pl.ds(start, rows)], from_plane.at[k, step - 1],
                      r3_send.at[k, step - 1], r3_recv.at[k, step - 1],
                      index(other_plane(step), peer, core))

    @pl.loop(0, downs + 5)
    def _(i):
        @pl.when(i < downs)
        def _():
            down_copy(i).wait()
            value = jnp.dot(hidden_buf[...], down_buf[i], preferred_element_type=F32)
            part[i] = (value * factor_buf[:, 0:1]).astype(BF)
            r1(i).start()

        @pl.when((i >= 1) & (i < downs + 1))
        def _():
            k = i - 1
            r1(k).wait_recv()
            part[k, pl.ds(base, half)] = (
                part[k, pl.ds(base, half)].astype(F32) + from_core[k].astype(F32)
            ).astype(BF)
            for j in range(1, peers):
                r2(k, j).start()

        @pl.when((i >= 3) & (i < downs + 3))
        def _():
            k = i - 3
            total = part[k, pl.ds(mine, span)].astype(F32)
            for j in range(1, peers):
                r2(k, j).wait_recv()
                total = total + from_peer[k, j - 1].astype(F32)
            part[k, pl.ds(mine, span)] = total.astype(BF)
            for step in range(1, experts):
                r3(k, step).start()

        @pl.when(i >= 5)
        def _():
            k = i - 5
            cols = pl.ds(pl.multiple_of(k * down_tile, down_tile), down_tile)
            total = part[k, pl.ds(final, rows)].astype(F32)
            for step in range(1, experts):
                r3(k, step).wait_recv()
                total = total + from_plane[k, step - 1].astype(F32)
            out_ref[:, cols] = (hid_ref[:, cols].astype(F32) + total).astype(BF)

    for step in range(1, experts):
        d1(step).wait_send()
    for step in range(experts):
        for j in range(1, peers):
            d2(j, step).wait_send()
        for j in range(peers):
            d3(j, step).wait_send()

    @pl.loop(0, downs)
    def _(k):
        r1(k).wait_send()
        for j in range(1, peers):
            r2(k, j).wait_send()
        for step in range(1, experts):
            r3(k, step).wait_send()


def per_device(hidden_in, norm_gain, router_weight, expert_ids, up_weight, down_weight):
    devices = lax.axis_size("expert")
    experts = router_weight.shape[1]
    peers = devices // experts // 2
    rows, width = hidden_in.shape
    depth = up_weight.shape[1]
    up_tile, down_tile = tile_of(depth), tile_of(width)
    ups, downs = depth // up_tile, width // down_tile
    whole = devices * rows
    dma = pltpu.SemaphoreType.DMA
    vmem = pl.BlockSpec(memory_space=pltpu.VMEM)
    return pl.pallas_call(
        functools.partial(kernel, devices, experts),
        out_shape=jax.ShapeDtypeStruct((rows, width), BF),
        in_specs=[vmem] * 4 + [pl.BlockSpec(memory_space=pl.ANY)] * 2,
        out_specs=vmem,
        scratch_shapes=[
            pltpu.VMEM((whole, width + EXTRA), BF),
            pltpu.VMEM((ups, width, up_tile), BF),
            pltpu.VMEM((downs, depth, down_tile), BF),
            pltpu.VMEM((whole, depth), BF),
            pltpu.VMEM((downs, whole, down_tile), BF),
            pltpu.VMEM((downs, whole // 2, down_tile), BF),
            pltpu.VMEM((downs, max(peers - 1, 1), experts * rows, down_tile), BF),
            pltpu.VMEM((downs, experts - 1, rows, down_tile), BF),
            pltpu.VMEM((whole, 128), F32),
            dma((ups,)), dma((downs,)),
            dma((experts - 1,)), dma((experts - 1,)),
            dma((max(peers - 1, 1), experts)), dma((max(peers - 1, 1), experts)),
            dma((peers, experts)), dma((peers, experts)),
            dma((downs,)), dma((downs,)),
            dma((downs, max(peers - 1, 1))), dma((downs, max(peers - 1, 1))),
            dma((downs, experts - 1)), dma((downs, experts - 1)),
        ],
        compiler_params=pltpu.CompilerParams(
            collective_id=0, has_side_effects=True, vmem_limit_bytes=62 * 1024 * 1024
        ),
        cost_estimate=pl.CostEstimate(
            flops=4 * whole * width * depth, bytes_accessed=4 * width * depth, transcendentals=whole * depth
        ),
    )(hidden_in, norm_gain[None, :], router_weight.T, expert_ids, up_weight, down_weight)


def solution(mesh):
    placed = (
        P(("groups", "expert"), None),
        P(),
        P(),
        P(("groups", "expert"), None),
        P(None, "expert"),
        P("expert", None),
    )
    return jax.shard_map(
        per_device,
        mesh=mesh,
        in_specs=placed,
        out_specs=P(("groups", "expert"), None),
        check_vma=False,
    )
```

```python
import functools

import jax
import jax.numpy as jnp
from jax import lax
from jax.experimental import pallas as pl
from jax.experimental.pallas import tpu as pltpu
from jax.sharding import PartitionSpec as P

MESH = pl.DeviceIdType.MESH
BF = jnp.bfloat16
F32 = jnp.float32
EXTRA = 128
CHUNKS = 4


def tile_of(size):
    for tile in (512, 384, 256, 128):
        if size % tile == 0:
            return tile
    return size


def kernel(
    devices, experts, hid_ref, gain_ref, router_ref, ids_ref, up_ref, down_ref, out_ref,
    rows_buf, up_buf, down_buf, hidden_buf, part, from_core, from_peer, from_plane, factor_buf, sums,
    up_sem, down_sem, d1_send, d1_recv, d2_send, d2_recv, d3_send, d3_recv,
    r1_send, r1_recv, r2_send, r2_recv, r3_send, r3_recv,
):
    group = devices // experts
    peers = group // 2
    rows, width = hid_ref.shape
    ups, _, up_tile = up_buf.shape
    downs, _, down_tile = down_buf.shape
    half = experts * peers * rows
    span = experts * rows
    me = lax.axis_index("expert")
    plane = me // group
    peer = lax.rem(me, group) // 2
    core = lax.rem(me, 2)

    def index(p, h, c):
        return p * group + h * 2 + c

    def place(p, h, c):
        return pl.multiple_of(((c * peers + h) * experts + p) * rows, rows)

    def other_plane(step):
        return lax.rem(plane + step, experts)

    def source_plane(step):
        return lax.rem(plane + experts - step, experts)

    def other_peer(step):
        return lax.rem(peer + step, peers)

    def source_peer(step):
        return lax.rem(peer + peers - step, peers)

    def remote(src, dst, send, recv, target):
        return pltpu.make_async_remote_copy(
            src_ref=src, dst_ref=dst, send_sem=send, recv_sem=recv,
            device_id={"expert": target}, device_id_type=MESH,
        )

    def up_copy(i):
        return pltpu.make_async_copy(
            up_ref.at[:, pl.ds(pl.multiple_of(i * up_tile, up_tile), up_tile)], up_buf.at[i], up_sem.at[i]
        )

    def down_copy(i):
        return pltpu.make_async_copy(
            down_ref.at[:, pl.ds(pl.multiple_of(i * down_tile, down_tile), down_tile)],
            down_buf.at[i], down_sem.at[i],
        )

    barrier = pltpu.get_barrier_semaphore()
    friends = [index(other_plane(s), peer, core) for s in range(1, experts)]
    friends += [index(plane, other_peer(s), core) for s in range(1, peers)]
    friends += [index(plane, peer, 1 - core)]
    for friend in friends:
        pl.semaphore_signal(barrier, inc=1, device_id={"expert": friend}, device_id_type=MESH)

    for i in range(ups):
        up_copy(i).start()
    for i in range(downs):
        down_copy(i).start()

    values = hid_ref[...].astype(F32)
    scale = lax.rsqrt(jnp.mean(values * values, axis=1, keepdims=True) + 1e-05)
    normed = (values * scale * gain_ref[...]).astype(BF)
    own = pl.ds(place(plane, peer, core), rows)
    rows_buf[own, :width] = normed
    normed32 = normed.astype(F32)
    router = router_ref[...].astype(F32)
    logits = [jnp.sum(normed32 * router[e:e + 1, :], axis=1, keepdims=True) for e in range(experts)]
    square = (rows, rows)
    eye = lax.broadcasted_iota(jnp.int32, square, 0) == lax.broadcasted_iota(jnp.int32, square, 1)
    ids_rows = ids_ref[...].astype(F32)
    first, second = [
        jnp.sum(jnp.where(eye, ids_rows[k:k + 1, :], 0.0), axis=1, keepdims=True).astype(jnp.int32)
        for k in range(2)
    ]
    picked = [
        sum(jnp.where(ids == e, logits[e], 0.0) for e in range(experts)) for ids in (first, second)
    ]
    mix0 = 1.0 / (1.0 + jnp.exp(picked[1] - picked[0]))
    mix1 = 1.0 / (1.0 + jnp.exp(picked[0] - picked[1]))
    lane = lax.broadcasted_iota(jnp.int32, (rows, EXTRA), 1)
    label = lax.rem(lane, experts)
    factor = jnp.where(first == label, mix0, 0.0) + jnp.where(second == label, mix1, 0.0)
    high = factor.astype(BF)
    low = (factor - high.astype(F32)).astype(BF)
    rows_buf[own, width:] = jnp.where(
        lane < experts, high.astype(F32), jnp.where(lane < 2 * experts, low.astype(F32), 0.0)
    ).astype(BF)

    pl.semaphore_wait(barrier, len(friends))

    depth_tile = width // CHUNKS

    def block(p, h, c, q):
        cols = depth_tile + (EXTRA if q == CHUNKS - 1 else 0)
        return rows_buf.at[pl.ds(place(p, h, c), rows), pl.ds(q * depth_tile, cols)]

    def d1(q, step):
        b = block(plane, peer, core, q)
        return remote(b, b, d1_send.at[q, step - 1], d1_recv.at[q, step - 1],
                      index(other_plane(step), peer, core))

    def d2(q, j, step):
        b = block(source_plane(step), peer, core, q)
        return remote(b, b, d2_send.at[q, j - 1, step], d2_recv.at[q, j - 1, step],
                      index(plane, other_peer(j), core))

    def d3(q, j, step):
        b = block(source_plane(step), source_peer(j), core, q)
        return remote(b, b, d3_send.at[q, j, step], d3_recv.at[q, j, step],
                      index(plane, peer, 1 - core))

    def pass_on_planes(q):
        for step in range(experts):
            if step:
                d1(q, step).wait_recv()
            for j in range(1, peers):
                d2(q, j, step).start()
            d3(q, 0, step).start()

    def pass_on_peers(q):
        for step in range(experts):
            for j in range(1, peers):
                d2(q, j, step).wait_recv()
                d3(q, j, step).start()

    def multiply(q):
        for step in range(experts):
            for j in range(peers):
                d3(q, j, step).wait_recv()
        span_q = slice(q * depth_tile, (q + 1) * depth_tile)

        @pl.loop(0, ups)
        def _(i):
            if q == 0:
                up_copy(i).wait()
            value = jnp.dot(rows_buf[:, span_q], up_buf[i, span_q, :], preferred_element_type=F32)
            if q:
                value = sums[i] + value
            if q < CHUNKS - 1:
                sums[i] = value
            else:
                hidden_buf[:, pl.ds(pl.multiple_of(i * up_tile, up_tile), up_tile)] = (
                    value / (1.0 + jnp.exp(-value))
                ).astype(BF)

    for q in range(CHUNKS):
        for step in range(1, experts):
            d1(q, step).start()
    pass_on_planes(0)
    for q in range(CHUNKS):
        if q + 1 < CHUNKS:
            pass_on_planes(q + 1)
        pass_on_peers(q)
        if q:
            multiply(q - 1)
    multiply(CHUNKS - 1)

    lane_all = lax.broadcasted_iota(jnp.int32, (2 * half, EXTRA), 1)
    chosen = (lane_all == plane) | (lane_all == plane + experts)
    factor_buf[...] = jnp.broadcast_to(
        jnp.sum(jnp.where(chosen, rows_buf[:, width:].astype(F32), 0.0), axis=1, keepdims=True),
        factor_buf.shape,
    )

    base = pl.multiple_of(core * half, rows)
    away = pl.multiple_of((1 - core) * half, rows)
    mine = pl.multiple_of(base + peer * span, rows)
    final = pl.multiple_of(mine + plane * rows, rows)

    def r1(k):
        return remote(part.at[k, pl.ds(away, half)], from_core.at[k], r1_send.at[k], r1_recv.at[k],
                      index(plane, peer, 1 - core))

    def r2(k, j):
        start = pl.multiple_of(base + other_peer(j) * span, rows)
        return remote(part.at[k, pl.ds(start, span)], from_peer.at[k, j - 1],
                      r2_send.at[k, j - 1], r2_recv.at[k, j - 1],
                      index(plane, other_peer(j), core))

    def r3(k, step):
        start = pl.multiple_of(mine + other_plane(step) * rows, rows)
        return remote(part.at[k, pl.ds(start, rows)], from_plane.at[k, step - 1],
                      r3_send.at[k, step - 1], r3_recv.at[k, step - 1],
                      index(other_plane(step), peer, core))

    @pl.loop(0, downs + 5)
    def _(i):
        @pl.when(i < downs)
        def _():
            down_copy(i).wait()
            value = jnp.dot(hidden_buf[...], down_buf[i], preferred_element_type=F32)
            part[i] = (value * factor_buf[:, 0:1]).astype(BF)
            r1(i).start()

        @pl.when((i >= 1) & (i < downs + 1))
        def _():
            k = i - 1
            r1(k).wait_recv()
            part[k, pl.ds(base, half)] = (
                part[k, pl.ds(base, half)].astype(F32) + from_core[k].astype(F32)
            ).astype(BF)
            for j in range(1, peers):
                r2(k, j).start()

        @pl.when((i >= 3) & (i < downs + 3))
        def _():
            k = i - 3
            total = part[k, pl.ds(mine, span)].astype(F32)
            for j in range(1, peers):
                r2(k, j).wait_recv()
                total = total + from_peer[k, j - 1].astype(F32)
            part[k, pl.ds(mine, span)] = total.astype(BF)
            for step in range(1, experts):
                r3(k, step).start()

        @pl.when(i >= 5)
        def _():
            k = i - 5
            cols = pl.ds(pl.multiple_of(k * down_tile, down_tile), down_tile)
            total = part[k, pl.ds(final, rows)].astype(F32)
            for step in range(1, experts):
                r3(k, step).wait_recv()
                total = total + from_plane[k, step - 1].astype(F32)
            out_ref[:, cols] = (hid_ref[:, cols].astype(F32) + total).astype(BF)

    for q in range(CHUNKS):
        for step in range(1, experts):
            d1(q, step).wait_send()
        for step in range(experts):
            for j in range(1, peers):
                d2(q, j, step).wait_send()
            for j in range(peers):
                d3(q, j, step).wait_send()

    @pl.loop(0, downs)
    def _(k):
        r1(k).wait_send()
        for j in range(1, peers):
            r2(k, j).wait_send()
        for step in range(1, experts):
            r3(k, step).wait_send()


def per_device(hidden_in, norm_gain, router_weight, expert_ids, up_weight, down_weight):
    devices = lax.axis_size("expert")
    experts = router_weight.shape[1]
    peers = devices // experts // 2
    rows, width = hidden_in.shape
    depth = up_weight.shape[1]
    up_tile, down_tile = tile_of(depth), tile_of(width)
    ups, downs = depth // up_tile, width // down_tile
    whole = devices * rows
    dma = pltpu.SemaphoreType.DMA
    vmem = pl.BlockSpec(memory_space=pltpu.VMEM)
    return pl.pallas_call(
        functools.partial(kernel, devices, experts),
        out_shape=jax.ShapeDtypeStruct((rows, width), BF),
        in_specs=[vmem] * 4 + [pl.BlockSpec(memory_space=pl.ANY)] * 2,
        out_specs=vmem,
        scratch_shapes=[
            pltpu.VMEM((whole, width + EXTRA), BF),
            pltpu.VMEM((ups, width, up_tile), BF),
            pltpu.VMEM((downs, depth, down_tile), BF),
            pltpu.VMEM((whole, depth), BF),
            pltpu.VMEM((downs, whole, down_tile), BF),
            pltpu.VMEM((downs, whole // 2, down_tile), BF),
            pltpu.VMEM((downs, max(peers - 1, 1), experts * rows, down_tile), BF),
            pltpu.VMEM((downs, experts - 1, rows, down_tile), BF),
            pltpu.VMEM((whole, 128), F32),
            pltpu.VMEM((ups, whole, up_tile), F32),
            dma((ups,)), dma((downs,)),
            dma((CHUNKS, experts - 1)), dma((CHUNKS, experts - 1)),
            dma((CHUNKS, max(peers - 1, 1), experts)), dma((CHUNKS, max(peers - 1, 1), experts)),
            dma((CHUNKS, peers, experts)), dma((CHUNKS, peers, experts)),
            dma((downs,)), dma((downs,)),
            dma((downs, max(peers - 1, 1))), dma((downs, max(peers - 1, 1))),
            dma((downs, experts - 1)), dma((downs, experts - 1)),
        ],
        compiler_params=pltpu.CompilerParams(
            collective_id=0, has_side_effects=True, vmem_limit_bytes=63 * 1024 * 1024
        ),
        cost_estimate=pl.CostEstimate(
            flops=4 * whole * width * depth, bytes_accessed=4 * width * depth, transcendentals=whole * depth
        ),
    )(hidden_in, norm_gain[None, :], router_weight.T, expert_ids.T, up_weight, down_weight)


def solution(mesh):
    placed = (
        P(("groups", "expert"), None),
        P(),
        P(),
        P(("groups", "expert"), None),
        P(None, "expert"),
        P("expert", None),
    )
    return jax.shard_map(
        per_device,
        mesh=mesh,
        in_specs=placed,
        out_specs=P(("groups", "expert"), None),
        check_vma=False,
    )
```

```python
import functools

import jax
import jax.numpy as jnp
from jax import lax
from jax.experimental import pallas as pl
from jax.experimental.pallas import tpu as pltpu
from jax.sharding import PartitionSpec as P

MESH = pl.DeviceIdType.MESH
BF = jnp.bfloat16
F32 = jnp.float32
EXTRA = 128
CHUNKS = 4
WINDOW = 2


def tile_of(size):
    for tile in (512, 384, 256, 128):
        if size % tile == 0:
            return tile
    return size


def kernel(
    devices, experts, hid_ref, gain_ref, router_ref, ids_ref, up_ref, down_ref, out_ref,
    rows_buf, up_buf, down_buf, hidden_buf, part, from_core, from_peer, from_plane, factor_buf, sums,
    up_sem, down_sem, d1_send, d1_recv, d2_send, d2_recv, d3_send, d3_recv,
    r1_send, r1_recv, r2_send, r2_recv, r3_send, r3_recv,
):
    group = devices // experts
    peers = group // 2
    rows, width = hid_ref.shape
    ups, _, up_tile = up_buf.shape
    downs, _, down_tile = down_buf.shape
    half = experts * peers * rows
    span = experts * rows
    me = lax.axis_index("expert")
    plane = me // group
    peer = lax.rem(me, group) // 2
    core = lax.rem(me, 2)

    def index(p, h, c):
        return p * group + h * 2 + c

    def place(p, h, c):
        return pl.multiple_of(((c * peers + h) * experts + p) * rows, rows)

    def other_plane(step):
        return lax.rem(plane + step, experts)

    def source_plane(step):
        return lax.rem(plane + experts - step, experts)

    def other_peer(step):
        return lax.rem(peer + step, peers)

    def source_peer(step):
        return lax.rem(peer + peers - step, peers)

    def remote(src, dst, send, recv, target):
        return pltpu.make_async_remote_copy(
            src_ref=src, dst_ref=dst, send_sem=send, recv_sem=recv,
            device_id={"expert": target}, device_id_type=MESH,
        )

    def up_copy(i):
        return pltpu.make_async_copy(
            up_ref.at[:, pl.ds(pl.multiple_of(i * up_tile, up_tile), up_tile)], up_buf.at[i], up_sem.at[i]
        )

    def down_copy(i):
        return pltpu.make_async_copy(
            down_ref.at[:, pl.ds(pl.multiple_of(i * down_tile, down_tile), down_tile)],
            down_buf.at[i], down_sem.at[i],
        )

    barrier = pltpu.get_barrier_semaphore()
    friends = [index(other_plane(s), peer, core) for s in range(1, experts)]
    friends += [index(plane, other_peer(s), core) for s in range(1, peers)]
    friends += [index(plane, peer, 1 - core)]
    for friend in friends:
        pl.semaphore_signal(barrier, inc=1, device_id={"expert": friend}, device_id_type=MESH)

    for i in range(ups):
        up_copy(i).start()
    for i in range(downs):
        down_copy(i).start()

    values = hid_ref[...].astype(F32)
    scale = lax.rsqrt(jnp.mean(values * values, axis=1, keepdims=True) + 1e-05)
    normed = (values * scale * gain_ref[...]).astype(BF)
    own = pl.ds(place(plane, peer, core), rows)
    rows_buf[own, :width] = normed
    normed32 = normed.astype(F32)
    router = router_ref[...].astype(F32)
    logits = [jnp.sum(normed32 * router[e:e + 1, :], axis=1, keepdims=True) for e in range(experts)]
    square = (rows, rows)
    eye = lax.broadcasted_iota(jnp.int32, square, 0) == lax.broadcasted_iota(jnp.int32, square, 1)
    ids_rows = ids_ref[...].astype(F32)
    first, second = [
        jnp.sum(jnp.where(eye, ids_rows[k:k + 1, :], 0.0), axis=1, keepdims=True).astype(jnp.int32)
        for k in range(2)
    ]
    picked = [
        sum(jnp.where(ids == e, logits[e], 0.0) for e in range(experts)) for ids in (first, second)
    ]
    mix0 = 1.0 / (1.0 + jnp.exp(picked[1] - picked[0]))
    mix1 = 1.0 / (1.0 + jnp.exp(picked[0] - picked[1]))
    lane = lax.broadcasted_iota(jnp.int32, (rows, EXTRA), 1)
    label = lax.rem(lane, experts)
    factor = jnp.where(first == label, mix0, 0.0) + jnp.where(second == label, mix1, 0.0)
    high = factor.astype(BF)
    low = (factor - high.astype(F32)).astype(BF)
    rows_buf[own, width:] = jnp.where(
        lane < experts, high.astype(F32), jnp.where(lane < 2 * experts, low.astype(F32), 0.0)
    ).astype(BF)

    pl.semaphore_wait(barrier, len(friends))

    depth_tile = width // CHUNKS

    def block(p, h, c, q):
        cols = depth_tile + (EXTRA if q == CHUNKS - 1 else 0)
        return rows_buf.at[pl.ds(place(p, h, c), rows), pl.ds(q * depth_tile, cols)]

    def d1(q, step):
        b = block(plane, peer, core, q)
        return remote(b, b, d1_send.at[q, step - 1], d1_recv.at[q, step - 1],
                      index(other_plane(step), peer, core))

    def d2(q, j, step):
        b = block(source_plane(step), peer, core, q)
        return remote(b, b, d2_send.at[q, j - 1, step], d2_recv.at[q, j - 1, step],
                      index(plane, other_peer(j), core))

    def d3(q, j, step):
        b = block(source_plane(step), source_peer(j), core, q)
        return remote(b, b, d3_send.at[q, j, step], d3_recv.at[q, j, step],
                      index(plane, peer, 1 - core))

    def pass_on_planes(q):
        for step in range(experts):
            if step:
                d1(q, step).wait_recv()
            for j in range(1, peers):
                d2(q, j, step).start()
            d3(q, 0, step).start()
        if q + WINDOW < CHUNKS:
            for step in range(1, experts):
                d1(q + WINDOW, step).start()

    def pass_on_peers(q):
        for step in range(experts):
            for j in range(1, peers):
                d2(q, j, step).wait_recv()
                d3(q, j, step).start()

    def multiply(q):
        for step in range(experts):
            for j in range(peers):
                d3(q, j, step).wait_recv()
        span_q = slice(q * depth_tile, (q + 1) * depth_tile)

        @pl.loop(0, ups)
        def _(i):
            if q == 0:
                up_copy(i).wait()
            value = jnp.dot(rows_buf[:, span_q], up_buf[i, span_q, :], preferred_element_type=F32)
            if q:
                value = sums[i] + value
            if q < CHUNKS - 1:
                sums[i] = value
            else:
                hidden_buf[:, pl.ds(pl.multiple_of(i * up_tile, up_tile), up_tile)] = (
                    value / (1.0 + jnp.exp(-value))
                ).astype(BF)

    for q in range(WINDOW):
        for step in range(1, experts):
            d1(q, step).start()
    pass_on_planes(0)
    for q in range(CHUNKS):
        if q + 1 < CHUNKS:
            pass_on_planes(q + 1)
        pass_on_peers(q)
        if q:
            multiply(q - 1)
    multiply(CHUNKS - 1)

    lane_all = lax.broadcasted_iota(jnp.int32, (2 * half, EXTRA), 1)
    chosen = (lane_all == plane) | (lane_all == plane + experts)
    factor_buf[...] = jnp.broadcast_to(
        jnp.sum(jnp.where(chosen, rows_buf[:, width:].astype(F32), 0.0), axis=1, keepdims=True),
        factor_buf.shape,
    )

    base = pl.multiple_of(core * half, rows)
    away = pl.multiple_of((1 - core) * half, rows)
    mine = pl.multiple_of(base + peer * span, rows)
    final = pl.multiple_of(mine + plane * rows, rows)

    def r1(k):
        return remote(part.at[k, pl.ds(away, half)], from_core.at[k], r1_send.at[k], r1_recv.at[k],
                      index(plane, peer, 1 - core))

    def r2(k, j):
        start = pl.multiple_of(base + other_peer(j) * span, rows)
        return remote(part.at[k, pl.ds(start, span)], from_peer.at[k, j - 1],
                      r2_send.at[k, j - 1], r2_recv.at[k, j - 1],
                      index(plane, other_peer(j), core))

    def r3(k, step):
        start = pl.multiple_of(mine + other_plane(step) * rows, rows)
        return remote(part.at[k, pl.ds(start, rows)], from_plane.at[k, step - 1],
                      r3_send.at[k, step - 1], r3_recv.at[k, step - 1],
                      index(other_plane(step), peer, core))

    @pl.loop(0, downs + 8)
    def _(i):
        @pl.when(i < downs)
        def _():
            down_copy(i).wait()
            value = jnp.dot(hidden_buf[...], down_buf[i], preferred_element_type=F32)
            part[i] = (value * factor_buf[:, 0:1]).astype(BF)
            r1(i).start()

        @pl.when((i >= 2) & (i < downs + 2))
        def _():
            k = i - 2
            r1(k).wait_recv()
            part[k, pl.ds(base, half)] = (
                part[k, pl.ds(base, half)].astype(F32) + from_core[k].astype(F32)
            ).astype(BF)
            for j in range(1, peers):
                r2(k, j).start()

        @pl.when((i >= 5) & (i < downs + 5))
        def _():
            k = i - 5
            total = part[k, pl.ds(mine, span)].astype(F32)
            for j in range(1, peers):
                r2(k, j).wait_recv()
                total = total + from_peer[k, j - 1].astype(F32)
            part[k, pl.ds(mine, span)] = total.astype(BF)
            for step in range(1, experts):
                r3(k, step).start()

        @pl.when(i >= 8)
        def _():
            k = i - 8
            cols = pl.ds(pl.multiple_of(k * down_tile, down_tile), down_tile)
            total = part[k, pl.ds(final, rows)].astype(F32)
            for step in range(1, experts):
                r3(k, step).wait_recv()
                total = total + from_plane[k, step - 1].astype(F32)
            out_ref[:, cols] = (hid_ref[:, cols].astype(F32) + total).astype(BF)

    for q in range(CHUNKS):
        for step in range(1, experts):
            d1(q, step).wait_send()
        for step in range(experts):
            for j in range(1, peers):
                d2(q, j, step).wait_send()
            for j in range(peers):
                d3(q, j, step).wait_send()

    @pl.loop(0, downs)
    def _(k):
        r1(k).wait_send()
        for j in range(1, peers):
            r2(k, j).wait_send()
        for step in range(1, experts):
            r3(k, step).wait_send()


def per_device(hidden_in, norm_gain, router_weight, expert_ids, up_weight, down_weight):
    devices = lax.axis_size("expert")
    experts = router_weight.shape[1]
    peers = devices // experts // 2
    rows, width = hidden_in.shape
    depth = up_weight.shape[1]
    up_tile, down_tile = tile_of(depth), tile_of(width)
    ups, downs = depth // up_tile, width // down_tile
    whole = devices * rows
    dma = pltpu.SemaphoreType.DMA
    vmem = pl.BlockSpec(memory_space=pltpu.VMEM)
    return pl.pallas_call(
        functools.partial(kernel, devices, experts),
        out_shape=jax.ShapeDtypeStruct((rows, width), BF),
        in_specs=[vmem] * 4 + [pl.BlockSpec(memory_space=pl.ANY)] * 2,
        out_specs=vmem,
        scratch_shapes=[
            pltpu.VMEM((whole, width + EXTRA), BF),
            pltpu.VMEM((ups, width, up_tile), BF),
            pltpu.VMEM((downs, depth, down_tile), BF),
            pltpu.VMEM((whole, depth), BF),
            pltpu.VMEM((downs, whole, down_tile), BF),
            pltpu.VMEM((downs, whole // 2, down_tile), BF),
            pltpu.VMEM((downs, max(peers - 1, 1), experts * rows, down_tile), BF),
            pltpu.VMEM((downs, experts - 1, rows, down_tile), BF),
            pltpu.VMEM((whole, 128), F32),
            pltpu.VMEM((ups, whole, up_tile), F32),
            dma((ups,)), dma((downs,)),
            dma((CHUNKS, experts - 1)), dma((CHUNKS, experts - 1)),
            dma((CHUNKS, max(peers - 1, 1), experts)), dma((CHUNKS, max(peers - 1, 1), experts)),
            dma((CHUNKS, peers, experts)), dma((CHUNKS, peers, experts)),
            dma((downs,)), dma((downs,)),
            dma((downs, max(peers - 1, 1))), dma((downs, max(peers - 1, 1))),
            dma((downs, experts - 1)), dma((downs, experts - 1)),
        ],
        compiler_params=pltpu.CompilerParams(
            collective_id=0, has_side_effects=True, vmem_limit_bytes=63 * 1024 * 1024
        ),
        cost_estimate=pl.CostEstimate(
            flops=4 * whole * width * depth, bytes_accessed=4 * width * depth, transcendentals=whole * depth
        ),
    )(hidden_in, norm_gain[None, :], router_weight.T, expert_ids.T, up_weight, down_weight)


def solution(mesh):
    placed = (
        P(("groups", "expert"), None),
        P(),
        P(),
        P(("groups", "expert"), None),
        P(None, "expert"),
        P("expert", None),
    )
    return jax.shard_map(
        per_device,
        mesh=mesh,
        in_specs=placed,
        out_specs=P(("groups", "expert"), None),
        check_vma=False,
    )
```
